128 devices in a mesh: section: 8 (over y, core), expert: 16 (over z, x).
Axes of the slice: x: 4, y: 4, z: 4, core: 2. Of those that a mesh axis runs over, the one named last changes fastest.
Arguments:
- leaving: bfloat16 [8, 1024, 2048], P('section', 'expert'), may hold values from -6 to 6
- returning: bfloat16 [8, 1024, 2048], P('section', 'expert'), may hold values from -6 to 6
- saved: bfloat16 [8, 1024, 2048], P('section', 'expert'), may hold values from -6 to 6
- gain: float32 [8, 2048], P('section'), may hold values from 0.5 to 1.5
- w_gate: bfloat16 [8, 16, 2048, 768], P('section', 'expert'), may hold values from -0.125 to 0.125
- w_up: bfloat16 [8, 16, 2048, 768], P('section', 'expert'), may hold values from -0.125 to 0.125
- w_down: bfloat16 [8, 16, 768, 2048], P('section', 'expert'), may hold values from -0.21875 to 0.21875
- route_a: int32 [8, 1024, 8], P('section', 'expert'), may hold values from 0 to 15, all different within a row; in each aligned block of 64 rows (0 to 63, 64 to 127, ..., all dimensions but the last counted through in order) at most 40 rows name the same one
- gates_a: float32 [8, 1024, 8], P('section', 'expert'), may hold values from 0.02 to 0.25
- route_b: int32 [8, 1024, 8], P('section', 'expert'), may hold values from 0 to 15, all different within a row; in each aligned block of 64 rows (0 to 63, 64 to 127, ..., all dimensions but the last counted through in order) at most 40 rows name the same one
- gates_b: float32 [8, 1024, 8], P('section', 'expert'), may hold values from 0.02 to 0.25
Outputs:
- mixed: bfloat16 [8, 1024, 2048], P('section', 'expert')
- input_grad: bfloat16 [8, 1024, 2048], P('section', 'expert')
- grad_gate: bfloat16 [8, 16, 2048, 768], P('section', 'expert')
- grad_up: bfloat16 [8, 16, 2048, 768], P('section', 'expert')
- grad_down: bfloat16 [8, 16, 768, 2048], P('section', 'expert')
- grad_gain: float32 [8, 2048], P('section')
The draws below stay inside these ranges and needn't reach their ends.
Inputs may be any that keep to these rules, and one draw needn't show every extreme that they name: `route_a`: each row names 8 different experts. Among the 64 rows of one device, no expert is named by more than 40 rows, and in some such blocks one is named by exactly 40. `route_b`: each row names 8 different experts. Among the 64 rows of one device, no expert is named by more than 40 rows, and in some such blocks one is named by exactly 40.
All inputs are finite; a program needn't handle non-finite values.
Results may differ from the reference program's by a relative error of at most 0.0073.
Values may be sent and summed in bfloat16 or wider, within the bound.
No kernel may reach another device: no remote copies, remote signals or barrier semaphores. Data moves between devices by JAX's collectives and lax.ppermute only.
A program may use at most 128 MiB of HBM per device.

```python
import math
import jax
import jax.numpy as jnp
import numpy as np
from jax import lax

D = 2048
FF = 768
TOP = 8
TOK_MB = 64
SECTIONS = 8
EXPERTS = 16
TOKENS = 1024
CAP = 40
N_EXPERT = 16


def level_of(stream_key, extent, split, least, top_value):
    level = 1.0
    for axis_at, blocks in split:
        steps = jax.random.uniform(jax.random.fold_in(jax.random.fold_in(stream_key, 6), axis_at), (blocks,), jnp.float32, least / len(split), top_value / len(split))
        level = level * jnp.repeat(jnp.exp(steps), extent[axis_at] // blocks).reshape((-1,) + (1,) * (len(extent) - 1 - axis_at))
    return level


def routed_block(rng, own, number, rows, amount, top, bound, lean):
    sequence = jax.random.permutation(rng, amount)
    heavy_load, common = shares(amount, rows * top, bound, lean, True), shares(amount, rows * top, bound, lean, False)
    places = jnp.arange(amount)

    def named(lengths, turn):
        used = int((lengths > 0).sum())
        fixed = max(1, used // 4)
        moved = fixed + (places - fixed + turn * (used - fixed)) % max(1, amount - fixed)
        return jnp.zeros((amount,), jnp.int32).at[sequence[jnp.where(places < fixed, places, moved)]].set(jnp.asarray(lengths, jnp.int32))

    lengths = jnp.where(number % 4 == 0, named(heavy_load, number // 4), named(common, number - number // 4 - 1))
    mixed = jax.random.permutation(jax.random.fold_in(own, 3), amount)
    source_of, sink = mixed[0:amount // 2 * 2:2], mixed[1:amount // 2 * 2:2]
    margin = jnp.minimum(lengths[source_of] - 1, bound - lengths[sink]) // 2
    margin = jnp.where((source_of == sequence[0]) | (sink == sequence[0]) | (lengths[sink] == 0), 0, jnp.maximum(margin, 0))
    moved = jax.random.randint(jax.random.fold_in(own, 4), (amount // 2,), 0, 1 << 20) % (margin + 1)
    lengths = lengths.at[source_of].add(-moved).at[sink].add(moved)
    labels = jnp.searchsorted(jnp.cumsum(lengths), jnp.arange(rows * top), side="right").astype(jnp.int32)
    listing = labels.reshape(top, rows).T
    listing = listing[jax.random.permutation(jax.random.fold_in(own, 1), rows)]
    turn = jax.random.randint(jax.random.fold_in(own, 2), (rows, 1), 0, top)
    return jnp.take_along_axis(listing, (jnp.arange(top)[None, :] + turn) % top, axis=1)


def shares(number_of, total, reach, skew, full):
    loads = [(1 << 20) // math.isqrt(standing ** skew) + 1 for standing in range(1, number_of + 1)]
    largest = reach if full else min(reach, max(-(-total // number_of), total * loads[0] // sum(loads)))
    least = 1 if total - largest >= number_of - 1 else 0
    holding, spare = [largest] + [least] * (number_of - 1), total - largest - least * (number_of - 1)
    while spare > 0:
        movable = [i for i in range(1, number_of) if holding[i] < largest] or [i for i in range(1, number_of) if holding[i] < reach]
        mass, left = sum([loads[i] for i in movable]), spare
        for i in movable:
            addition = min(reach - holding[i], max(1, left * loads[i] // mass), spare)
            holding[i] = holding[i] + addition
            spare = spare - addition
    return np.array(holding)


def normal_values(stream_key, dims, width, most, pieces=(), held_as=jnp.bfloat16):
    loudness = level_of(stream_key, dims, pieces, -0.22, 0.18) if pieces else 1.0
    array = jax.random.normal(stream_key, dims, jnp.float32) * width * loudness
    return jnp.minimum(jnp.maximum(array, -most), most).astype(held_as)


def setup_inputs(seed: int = 0) -> dict:
    seeds = jax.random.split(jax.random.key(seed), 12)
    leaving = normal_values(seeds[0], (SECTIONS, TOKENS, D), 1.0, 6.0, ((0, 8), (1, 16)))
    returning = normal_values(seeds[1], (SECTIONS, TOKENS, D), 1.0, 6.0, ((0, 8), (1, 16)))
    saved = normal_values(seeds[2], (SECTIONS, TOKENS, D), 1.0, 6.0, ((0, 8), (1, 16)))
    gain = jnp.clip(1.0 + 0.1 * jax.random.normal(seeds[3], (SECTIONS, D), jnp.float32), 0.5, 1.5)
    w_gate = normal_values(seeds[4], (SECTIONS, EXPERTS, D, FF), D ** -0.5, 0.125, ((0, 8), (1, 16)))
    w_up = normal_values(seeds[5], (SECTIONS, EXPERTS, D, FF), D ** -0.5, 0.125, ((0, 8), (1, 16)))
    w_down = normal_values(seeds[6], (SECTIONS, EXPERTS, FF, D), FF ** -0.5, 0.21875, ((0, 8), (1, 16)))
    route_a_keys = jax.random.split(jax.random.fold_in(seeds[7], 1), SECTIONS * TOKENS // TOK_MB)
    route_a_turns = jax.random.permutation(jax.random.fold_in(seeds[7], 3), SECTIONS * TOKENS // TOK_MB)
    route_a = jax.vmap(lambda own, number: routed_block(jax.random.fold_in(seeds[7], 2), own, number, TOK_MB, EXPERTS, TOP, CAP, 2))(route_a_keys, route_a_turns).reshape((SECTIONS, TOKENS, TOP))
    gates_a = jnp.clip(0.02 + 0.23 * jax.random.uniform(seeds[8], (SECTIONS, TOKENS, TOP), jnp.float32) ** level_of(seeds[8], (SECTIONS, TOKENS, TOP), ((0, 8), (1, 16)), -0.2, 0.2), 0.02, 0.25)
    route_b_keys = jax.random.split(jax.random.fold_in(seeds[9], 1), SECTIONS * TOKENS // TOK_MB)
    route_b_turns = jax.random.permutation(jax.random.fold_in(seeds[9], 3), SECTIONS * TOKENS // TOK_MB)
    route_b = jax.vmap(lambda own, number: routed_block(jax.random.fold_in(seeds[9], 2), own, number, TOK_MB, EXPERTS, TOP, CAP, 2))(route_b_keys, route_b_turns).reshape((SECTIONS, TOKENS, TOP))
    gates_b = jnp.clip(0.02 + 0.23 * jax.random.uniform(seeds[10], (SECTIONS, TOKENS, TOP), jnp.float32) ** level_of(seeds[10], (SECTIONS, TOKENS, TOP), ((0, 8), (1, 16)), -0.2, 0.2), 0.02, 0.25)
    return dict(leaving=leaving, returning=returning, saved=saved, gain=gain, w_gate=w_gate, w_up=w_up, w_down=w_down, route_a=route_a, gates_a=gates_a, route_b=route_b, gates_b=gates_b)


epsilon = 1e-06

def contract(left, right, left_dim, right_dim):
    return lax.dot_general(left, right, (((left_dim,), (right_dim,)), ((), ())), preferred_element_type=jnp.float32)

def normalize(panel, gain_row):
    values = panel.astype(jnp.float32)
    scale = lax.rsqrt(lax.optimization_barrier(jnp.mean(values * values, axis=-1, keepdims=True)) + epsilon)
    unit = values * scale
    return (unit, scale, (unit * gain_row).astype(jnp.bfloat16))

def expert_forward(rows, gate_w, up_w, down_w):
    pre_gate = contract(rows, gate_w, 1, 0)
    pre_up = contract(rows, up_w, 1, 0)
    hidden = (pre_gate * jax.nn.sigmoid(pre_gate) * pre_up).astype(jnp.bfloat16)
    return contract(hidden, down_w, 1, 0).astype(jnp.bfloat16)

def expert_backward(rows, slot_grad, gate_w, up_w, down_w):
    pre_gate = contract(rows, gate_w, 1, 0)
    pre_up = contract(rows, up_w, 1, 0)
    sigma = jax.nn.sigmoid(pre_gate)
    activ = pre_gate * sigma
    hidden = (activ * pre_up).astype(jnp.bfloat16)
    hidden_grad = contract(slot_grad, down_w, 1, 1)
    gate_grad = (hidden_grad * pre_up * sigma * (1.0 + pre_gate * (1.0 - sigma))).astype(jnp.bfloat16)
    up_grad = (hidden_grad * activ).astype(jnp.bfloat16)
    row_grad = (contract(gate_grad, gate_w, 1, 1) + contract(up_grad, up_w, 1, 1)).astype(jnp.bfloat16)
    return (row_grad, contract(rows, gate_grad, 0, 0).astype(jnp.bfloat16), contract(rows, up_grad, 0, 0).astype(jnp.bfloat16), contract(hidden, slot_grad, 0, 0).astype(jnp.bfloat16))

def place_slots(route):
    blocks = route.reshape(N_EXPERT, TOK_MB * TOP)
    hits = (blocks[:, :, None] == jnp.arange(EXPERTS, dtype=jnp.int32)[None, None, :]).astype(jnp.int32)
    ranks = lax.optimization_barrier(jnp.sum((jnp.cumsum(hits, axis=1) - hits) * hits, axis=2))
    source = jnp.arange(N_EXPERT, dtype=jnp.int32)[:, None]
    return (blocks * (N_EXPERT * CAP) + source * CAP + ranks).astype(jnp.int32).reshape(TOKENS, TOP)

def dispatch(values, targets):
    buffer = jnp.zeros((EXPERTS * N_EXPERT * CAP, D), values.dtype)
    buffer = buffer.at[targets.reshape(-1)].set(values.reshape(-1, D))
    return buffer.reshape(EXPERTS, N_EXPERT * CAP, D)

def one_section(items):
    arrived, upstream, kept, gain_row, gate_w, up_w, down_w, route_one, gates_one, route_two, gates_two = items
    unused_unit, unused_scale, normed = normalize(arrived, gain_row)
    targets = place_slots(route_one)
    buffer = dispatch(jnp.broadcast_to(normed[:, None, :], (TOKENS, TOP, D)), targets)
    outputs = lax.map(lambda members: expert_forward(*members), (buffer, gate_w, up_w, down_w)).reshape(-1, D)
    mixed = (arrived.astype(jnp.float32) + lax.optimization_barrier(jnp.sum(gates_one[:, :, None] * outputs[targets].astype(jnp.float32), axis=1))).astype(jnp.bfloat16)
    unit, scale, normed_two = normalize(kept, gain_row)
    targets_two = place_slots(route_two)
    rows_two = dispatch(jnp.broadcast_to(normed_two[:, None, :], (TOKENS, TOP, D)), targets_two)
    upstream_f = upstream.astype(jnp.float32)
    slot_grads = (gates_two[:, :, None] * upstream_f[:, None, :]).astype(jnp.bfloat16)
    grads_buffer = dispatch(slot_grads, targets_two)
    row_grads, grad_gate, grad_up, grad_down = lax.map(lambda members: expert_backward(*members), (rows_two, grads_buffer, gate_w, up_w, down_w))
    normed_grad = lax.optimization_barrier(jnp.sum(row_grads.reshape(-1, D)[targets_two].astype(jnp.float32), axis=1))
    scaled = normed_grad * gain_row
    input_grad = (upstream_f + scale * (scaled - unit * lax.optimization_barrier(jnp.mean(scaled * unit, axis=-1, keepdims=True)))).astype(jnp.bfloat16)
    gain_grad = lax.optimization_barrier(jnp.sum(normed_grad * unit, axis=0))
    return (mixed, input_grad, grad_gate, grad_up, grad_down, gain_grad)

def reference(leaving, returning, saved, gain, w_gate, w_up, w_down, route_a, gates_a, route_b, gates_b):
    arriving = jnp.roll(leaving, 1, axis=0)
    upstream = jnp.roll(returning, -1, axis=0)
    mixed, input_grad, grad_gate, grad_up, grad_down, grad_gain = lax.map(one_section, (arriving, upstream, saved, gain, w_gate, w_up, w_down, route_a, gates_a, route_b, gates_b))
    return (mixed, input_grad, grad_gate, grad_up, grad_down, grad_gain)
```

```python
import functools

import jax
import jax.numpy as jnp
from jax import lax
from jax.experimental import pallas as pl
from jax.experimental.pallas import tpu as pltpu
from jax.sharding import PartitionSpec as P

epsilon = 1e-06
SIDE = 4
LANES = 128
MIB = 1 << 20


def shifted(value, axis, steps):
    count = lax.axis_size(axis)
    pairs = [(source, (source + steps) % count) for source in range(count)]
    return lax.ppermute(value, axis, pairs)


def along_x(value, steps):
    pairs = [(z * SIDE + x, z * SIDE + (x + steps) % SIDE) for z in range(SIDE) for x in range(SIDE)]
    return lax.ppermute(value, "expert", pairs)


def along_z(value, steps):
    pairs = [(z * SIDE + x, (z + steps) % SIDE * SIDE + x) for z in range(SIDE) for x in range(SIDE)]
    return lax.ppermute(value, "expert", pairs)


def partnered(value, bit, count):
    return lax.ppermute(value, "expert", [(source, source ^ bit) for source in range(count)])


def contract(left, right, left_dim, right_dim):
    return lax.dot_general(
        left, right, (((left_dim,), (right_dim,)), ((), ())), preferred_element_type=jnp.float32
    )


def normalize(panel, gain_row):
    values = panel.astype(jnp.float32)
    scale = lax.rsqrt(jnp.mean(values * values, axis=-1, keepdims=True) + epsilon)
    unit = values * scale
    return (unit, scale, (unit * gain_row).astype(jnp.bfloat16))


def gather_near(block):
    half = block.shape[0] // 2
    first, second = lax.optimization_barrier((block[:half], block[half:]))
    near_first = (first, along_x(first, 1), along_x(first, -1), along_x(first, 2))
    near_second = (second, along_z(second, 1), along_z(second, -1), along_z(second, 2))
    return lax.optimization_barrier(
        (jnp.concatenate(near_first, axis=0), jnp.concatenate(near_second, axis=0))
    )


def gather_beside(first, second):
    return (along_z(first, 1), along_z(first, -1), along_x(second, 1), along_x(second, -1))


def gather_far(beside):
    low = beside[0].shape[0] // 2
    parts = lax.optimization_barrier(
        (beside[0][:low], beside[1][low:], beside[2][:low], beside[3][low:])
    )
    return (along_z(parts[0], 1), along_z(parts[1], -1), along_x(parts[2], 1), along_x(parts[3], -1))


def scatter_pieces(own, beside, far):
    own_first, own_second = own
    lower_first, upper_first, lower_second, upper_second = beside
    low_first, high_first, low_second, high_second = far
    got = (
        along_z(low_first, -1), along_z(high_first, 1), along_x(low_second, -1), along_x(high_second, 1)
    )

    def below(piece, part):
        return (
            piece.astype(jnp.float32) + jnp.pad(part, ((0, part.shape[0]), (0, 0))).astype(jnp.float32)
        ).astype(jnp.bfloat16)

    def above(piece, part):
        return (
            piece.astype(jnp.float32) + jnp.pad(part, ((part.shape[0], 0), (0, 0))).astype(jnp.float32)
        ).astype(jnp.bfloat16)

    sums = lax.optimization_barrier(
        (
            below(lower_first, got[0]), above(upper_first, got[1]),
            below(lower_second, got[2]), above(upper_second, got[3]),
        )
    )
    back = (along_z(sums[0], -1), along_z(sums[1], 1), along_x(sums[2], -1), along_x(sums[3], 1))
    total_first = own_first.astype(jnp.float32) + back[0].astype(jnp.float32) + back[1].astype(jnp.float32)
    total_second = own_second.astype(jnp.float32) + back[2].astype(jnp.float32) + back[3].astype(jnp.float32)
    rows = total_first.shape[0] // SIDE

    def parts(total):
        sent = total.astype(jnp.bfloat16)
        return total[:rows], sent[rows : 2 * rows], sent[2 * rows : 3 * rows], sent[3 * rows :]

    one = parts(total_first)
    two = parts(total_second)
    one, two = lax.optimization_barrier((one, two))
    first = (along_x(one[1], -1), along_x(one[2], 1), along_x(one[3], 2))
    second = (along_z(two[1], -1), along_z(two[2], 1), along_z(two[3], 2))
    sum_first = one[0] + sum(part.astype(jnp.float32) for part in first)
    sum_second = two[0] + sum(part.astype(jnp.float32) for part in second)
    return jnp.concatenate([sum_first, sum_second], axis=0)


def gate_columns(route_a, gates_a, route_b, gates_b, experts):
    names = jnp.arange(experts, dtype=jnp.int32)
    columns = []
    for route, gates in ((route_a, gates_a), (route_b, gates_b)):
        dense = jnp.sum(jnp.where(route[:, :, None] == names, gates[:, :, None], 0.0), axis=1)
        for turn in range(3):
            term = lax.reduce_precision(dense, 8, 7)
            columns.append(term.astype(jnp.bfloat16))
            dense = dense - term
    rows = route_a.shape[0]
    columns.append(jnp.zeros((rows, LANES - 6 * experts), jnp.bfloat16))
    return jnp.concatenate(columns, axis=1)


def expert_kernel(places, start, fresh, *refs):
    count = len(places) - 1
    pieces = refs[:count]
    gate_hbm, up_hbm, down_hbm, pick_ref = refs[count : count + 4]
    rest = refs[count + 4 + (0 if fresh else 5) :]
    outs = rest[:count]
    gain_out, rows_out, slots_out, hidden_out, da_out, du_out = rest[count : count + 6]
    (panel, slots, hidden, da, du, gate_w, up_w, down_w,
     piece_sems, weight_sems, out_sems) = rest[count + 6 :]
    width = gate_w.shape[0]
    loads = [
        pltpu.make_async_copy(
            pieces[i], panel.at[pl.ds(places[i], places[i + 1] - places[i])], piece_sems.at[i]
        )
        for i in range(count)
    ]
    weights = [
        pltpu.make_async_copy(source, target, weight_sems.at[i])
        for i, (source, target) in enumerate(((gate_hbm, gate_w), (up_hbm, up_w), (down_hbm, down_w)))
    ]
    for load in loads + weights:
        load.start()
    stores = []

    def keep(source, target):
        copy = pltpu.make_async_copy(
            source, target.at[pl.ds(start, places[-1])], out_sems.at[len(stores)]
        )
        copy.start()
        stores.append(copy)

    for load in loads:
        load.wait()
    keep(panel.at[:, pl.ds(0, width)], rows_out)
    gates = jnp.dot(panel[:, 3 * width :], pick_ref[...], preferred_element_type=jnp.float32)
    weights[0].wait()
    rows = panel[:, :width]
    pre_gate = jnp.dot(rows, gate_w[...], preferred_element_type=jnp.float32)
    slots[...] = (gates[:, 1:2] * panel[:, width : 2 * width].astype(jnp.float32)).astype(jnp.bfloat16)
    keep(slots, slots_out)
    weights[1].wait()
    pre_up = jnp.dot(rows, up_w[...], preferred_element_type=jnp.float32)
    weights[2].wait()
    hidden_grad = contract(slots[...], down_w[...], 1, 1)
    sigma = jax.nn.sigmoid(pre_gate)
    activ = pre_gate * sigma
    hidden[...] = (activ * pre_up).astype(jnp.bfloat16)
    keep(hidden, hidden_out)
    da[...] = (hidden_grad * pre_up * sigma * (1.0 + pre_gate * (1.0 - sigma))).astype(jnp.bfloat16)
    du[...] = (hidden_grad * activ).astype(jnp.bfloat16)
    keep(da, da_out)
    keep(du, du_out)
    back = contract(da[...], gate_w[...], 1, 1) + contract(du[...], up_w[...], 1, 1)
    gain_out[...] = jnp.sum(back * panel[:, :width].astype(jnp.float32), axis=0, keepdims=True)
    back = back.astype(jnp.bfloat16)
    for i in range(count):
        outs[i][:, :width] = back[places[i] : places[i + 1]]
    others = panel[:, 2 * width : 3 * width]
    pre_gate = jnp.dot(others, gate_w[...], preferred_element_type=jnp.float32)
    pre_up = jnp.dot(others, up_w[...], preferred_element_type=jnp.float32)
    ahead = (pre_gate * jax.nn.sigmoid(pre_gate) * pre_up).astype(jnp.bfloat16)
    out = jnp.dot(ahead, down_w[...], preferred_element_type=jnp.float32)
    out = (out * gates[:, 0:1]).astype(jnp.bfloat16)
    for i in range(count):
        outs[i][:, width:] = out[places[i] : places[i + 1]]
    for store in stores:
        store.wait()


def run_expert(pieces, gate_w, up_w, down_w, pick, kept, start, total):
    places = [0]
    for piece in pieces:
        places.append(places[-1] + piece.shape[0])
    rows, (width, hidden) = places[-1], gate_w.shape
    count = len(pieces)
    anywhere = pl.BlockSpec(memory_space=pl.ANY)
    here = pl.BlockSpec(memory_space=pltpu.VMEM)
    bf16 = jnp.bfloat16
    results = pl.pallas_call(
        functools.partial(expert_kernel, tuple(places), start, kept is None),
        out_shape=[jax.ShapeDtypeStruct((piece.shape[0], 2 * width), bf16) for piece in pieces]
        + [jax.ShapeDtypeStruct((1, width), jnp.float32)]
        + [jax.ShapeDtypeStruct((total, width), bf16)] * 2
        + [jax.ShapeDtypeStruct((total, hidden), bf16)] * 3,
        in_specs=[anywhere] * (count + 3) + [here] + ([] if kept is None else [anywhere] * 5),
        out_specs=[here] * (count + 1) + [anywhere] * 5,
        input_output_aliases={} if kept is None else {count + 4 + i: count + 1 + i for i in range(5)},
        scratch_shapes=[
            pltpu.VMEM((rows, pieces[0].shape[1]), bf16),
            pltpu.VMEM((rows, width), bf16),
            pltpu.VMEM((rows, hidden), bf16),
            pltpu.VMEM((rows, hidden), bf16),
            pltpu.VMEM((rows, hidden), bf16),
            pltpu.VMEM(gate_w.shape, bf16),
            pltpu.VMEM(up_w.shape, bf16),
            pltpu.VMEM(down_w.shape, bf16),
            pltpu.SemaphoreType.DMA((count,)),
            pltpu.SemaphoreType.DMA((3,)),
            pltpu.SemaphoreType.DMA((5,)),
        ],
        compiler_params=pltpu.CompilerParams(vmem_limit_bytes=52 * MIB),
        cost_estimate=pl.CostEstimate(
            flops=24 * rows * width * hidden, bytes_accessed=30 * MIB, transcendentals=2 * rows * hidden
        ),
        name="expert",
    )(*pieces, gate_w, up_w, down_w, pick, *(() if kept is None else kept))
    return results[:count], results[count], results[count + 1 :]


def per_device(
    leaving, returning, saved, gain, w_gate, w_up, w_down, route_a, gates_a, route_b, gates_b
):
    experts = lax.axis_size("expert")
    gain_row = gain[0]
    gate_w = w_gate[0, 0]
    up_w = w_up[0, 0]
    down_w = w_down[0, 0]
    upstream = shifted(returning, "section", -1)[0]
    arrived = shifted(leaving, "section", 1)[0]
    unit, scale, normed_two = normalize(saved[0], gain_row)
    columns = gate_columns(route_a[0], gates_a[0], route_b[0], gates_b[0], experts)
    line = jnp.arange(LANES, dtype=jnp.int32)
    pick = (
        (line[:, None] % experts == lax.axis_index("expert"))
        & (line[:, None] // (3 * experts) == line[None, :])
        & (line[None, :] < 2)
    ).astype(jnp.bfloat16)
    unused_unit, unused_scale, normed_one = normalize(arrived, gain_row)
    own = gather_near(jnp.concatenate([normed_two, upstream, normed_one, columns], axis=1))
    beside = gather_beside(*own)
    far = gather_far(beside)
    total = experts * upstream.shape[0]
    expert = functools.partial(
        run_expert, gate_w=gate_w, up_w=up_w, down_w=down_w, pick=pick, total=total
    )
    own_out, gain_own, kept = expert(own, kept=None, start=0)
    beside_out, gain_beside, kept = expert(beside, kept=kept, start=total // 4)
    far_out, gain_far, kept = expert(far, kept=kept, start=3 * total // 4)
    rows_b, slot_grad, hidden, gate_grad, up_grad = kept
    returned = scatter_pieces(own_out, beside_out, far_out)
    width = upstream.shape[1]
    normed_grad, gathered = returned[:, :width], returned[:, width:]
    grad_gate = contract(rows_b, gate_grad, 0, 0).astype(jnp.bfloat16)
    grad_up = contract(rows_b, up_grad, 0, 0).astype(jnp.bfloat16)
    grad_down = contract(hidden, slot_grad, 0, 0).astype(jnp.bfloat16)
    scaled = normed_grad * gain_row
    input_grad = (
        upstream.astype(jnp.float32)
        + scale * (scaled - unit * jnp.mean(scaled * unit, axis=-1, keepdims=True))
    ).astype(jnp.bfloat16)
    gain_total = (gain_own + gain_beside + gain_far) / gain
    for bit in range(experts.bit_length() - 1):
        gain_total = gain_total + partnered(gain_total, 1 << bit, experts)
    mixed = (arrived.astype(jnp.float32) + gathered).astype(jnp.bfloat16)
    return (
        mixed[None],
        input_grad[None],
        grad_gate[None, None],
        grad_up[None, None],
        grad_down[None, None],
        gain_total,
    )


def solution(mesh):
    placed = (
        P("section", "expert", None),
        P("section", "expert", None),
        P("section", "expert", None),
        P("section", None),
        P("section", "expert", None, None),
        P("section", "expert", None, None),
        P("section", "expert", None, None),
        P("section", "expert", None),
        P("section", "expert", None),
        P("section", "expert", None),
        P("section", "expert", None),
    )
    return jax.shard_map(
        per_device,
        mesh=mesh,
        in_specs=placed,
        out_specs=(
            P("section", "expert", None),
            P("section", "expert", None),
            P("section", "expert", None, None),
            P("section", "expert", None, None),
            P("section", "expert", None, None),
            P("section", None),
        ),
        check_vma=False,
    )
```

```python
import functools

import jax
import jax.numpy as jnp
from jax import lax
from jax.experimental import pallas as pl
from jax.experimental.pallas import tpu as pltpu
from jax.sharding import PartitionSpec as P

epsilon = 1e-06
SIDE = 4
LANES = 128
MIB = 1 << 20
SMALL = pl.CostEstimate(flops=1 << 20, bytes_accessed=1 << 16, transcendentals=0)


def shifted(value, axis, steps):
    count = lax.axis_size(axis)
    pairs = [(source, (source + steps) % count) for source in range(count)]
    return lax.ppermute(value, axis, pairs)


def along_x(value, steps):
    pairs = [(z * SIDE + x, z * SIDE + (x + steps) % SIDE) for z in range(SIDE) for x in range(SIDE)]
    return lax.ppermute(value, "expert", pairs)


def along_z(value, steps):
    pairs = [(z * SIDE + x, (z + steps) % SIDE * SIDE + x) for z in range(SIDE) for x in range(SIDE)]
    return lax.ppermute(value, "expert", pairs)


def contract(left, right, left_dim, right_dim):
    return lax.dot_general(
        left, right, (((left_dim,), (right_dim,)), ((), ())), preferred_element_type=jnp.float32
    )


def normalize(panel, gain_row):
    values = panel.astype(jnp.float32)
    scale = lax.rsqrt(jnp.mean(values * values, axis=-1, keepdims=True) + epsilon)
    unit = values * scale
    return (unit, scale, (unit * gain_row).astype(jnp.bfloat16))


def gather_near(block):
    half = block.shape[0] // 2
    first, second = block[:half], block[half:]
    near_first = (first, along_x(first, 1), along_x(first, -1), along_x(first, 2))
    near_second = (second, along_z(second, 1), along_z(second, -1), along_z(second, 2))
    return tuple(
        jnp.concatenate(pair, axis=0)
        for pair in (near_first[:2], near_first[2:], near_second[:2], near_second[2:])
    )


def gather_onward(near):
    return (along_z(near[0], 1), along_z(near[1], -1), along_x(near[2], 1), along_x(near[3], -1))


def gather_staying(near):
    return (along_z(near[1], 1), along_z(near[0], -1), along_x(near[3], 1), along_x(near[2], -1))


def gather_far(onward):
    return (along_z(onward[0], 1), along_z(onward[1], -1), along_x(onward[2], 1), along_x(onward[3], -1))


def scatter_far(far):
    return (along_z(far[0], -1), along_z(far[1], 1), along_x(far[2], -1), along_x(far[3], 1))


def scatter_staying(staying):
    return (along_z(staying[0], -1), along_z(staying[1], 1), along_x(staying[2], -1), along_x(staying[3], 1))


def added(*parts):
    total = parts[0].astype(jnp.float32)
    for part in parts[1:]:
        total = total + part.astype(jnp.float32)
    return total


def relayed(onward, far):
    return [added(mine, other).astype(jnp.bfloat16) for mine, other in zip(onward, far)]


def ring_sum(own, lower, upper, opposite):
    return (own + opposite) + (lower + upper)


def scatter_sums(near, sums, staid, extra):
    back = (along_z(sums[0], -1), along_z(sums[1], 1), along_x(sums[2], -1), along_x(sums[3], 1))
    totals = (
        added(near[0], back[0], staid[1]),
        added(near[1], back[1], staid[0]),
        added(near[2], back[2], staid[3]),
        added(near[3], back[3], staid[2]),
    )
    rows = totals[0].shape[0] // 2
    width = totals[0].shape[1]
    high = lax.reduce_precision(extra, 8, 7)
    terms = jnp.concatenate([high, lax.reduce_precision(extra - high, 8, 7)]).astype(jnp.bfloat16)
    terms = terms.reshape(rows, -1)

    def parts(own):
        lower, upper, opposite = own[0][rows:], own[1][:rows], own[1][rows:]
        return own[0][:rows], [part.astype(jnp.bfloat16) for part in (lower, upper, opposite)]

    def ends(sent, move):
        return move(sent[0], -1), move(sent[1], 1), move(sent[2], 2)

    own_first, sent_first = parts(totals[:2])
    own_second, sent_second = parts(totals[2:])
    sent_second = [jnp.concatenate([part, terms], axis=1) for part in sent_second]
    got_first = ends(sent_first, along_x)
    got_second = ends(sent_second, along_z)
    result = jnp.concatenate(
        [added(own_first, *got_first), added(own_second, *(part[:, :width] for part in got_second))], axis=0
    )

    def joined(columns):
        both = columns.astype(jnp.float32).reshape(2, -1)
        return both[:1] + both[1:]

    upper, lower, opposite = (joined(part[:, width:]) for part in got_second)
    return result, ring_sum(joined(terms), lower, upper, opposite)


def gate_columns(route_a, gates_a, route_b, gates_b, experts):
    names = jnp.arange(experts, dtype=jnp.int32)
    columns = []
    for route, gates in ((route_a, gates_a), (route_b, gates_b)):
        dense = jnp.sum(jnp.where(route[:, :, None] == names, gates[:, :, None], 0.0), axis=1)
        for turn in range(3):
            term = lax.reduce_precision(dense, 8, 7)
            columns.append(term.astype(jnp.bfloat16))
            dense = dense - term
    rows = route_a.shape[0]
    columns.append(jnp.zeros((rows, LANES - 6 * experts), jnp.bfloat16))
    return jnp.concatenate(columns, axis=1)


def expert_kernel(places, start, fresh, again, *refs):
    count = len(places) - 1
    pieces = refs[:count]
    gate_hbm, up_hbm, down_hbm, pick_ref = refs[count : count + 4]
    rest = refs[count + 4 + (0 if fresh else 5) :]
    outs = rest[:count]
    gain_out, rows_out, slots_out, hidden_out, da_out, du_out = rest[count : count + 6]
    repeats = rest[count + 6 : 2 * count + 6] if again else ()
    (panel, slots, hidden, da, du, gate_w, up_w, down_w,
     piece_sems, weight_sems, out_sems) = rest[-11:]
    width = gate_w.shape[0]
    def load(part, first, last):
        copies = []
        for i in range(count):
            here, columns = pl.ds(places[i], places[i + 1] - places[i]), pl.ds(first, last - first)
            copies.append(
                pltpu.make_async_copy(
                    pieces[i].at[:, columns], panel.at[here, columns], piece_sems.at[part * count + i]
                )
            )
        return copies

    loads = [load(0, 0, width), load(1, width, 2 * width), load(2, 2 * width, pieces[0].shape[1])]
    weights = [
        pltpu.make_async_copy(source, target, weight_sems.at[i])
        for i, (source, target) in enumerate(((gate_hbm, gate_w), (up_hbm, up_w), (down_hbm, down_w)))
    ]
    stores = []

    def store(source, target):
        copy = pltpu.make_async_copy(source, target, out_sems.at[len(stores)])
        copy.start()
        stores.append(copy)

    def keep(source, target):
        store(source, target.at[pl.ds(start, places[-1])])

    for copy in loads[0] + weights[:1]:
        copy.start()
    for copy in loads[0]:
        copy.wait()
    weights[1].start()
    weights[0].wait()
    for copy in loads[1] + loads[2] + weights[2:]:
        copy.start()
    pre_gate = jnp.dot(panel[:, :width], gate_w[...], preferred_element_type=jnp.float32)
    weights[1].wait()
    pre_up = jnp.dot(panel[:, :width], up_w[...], preferred_element_type=jnp.float32)
    for copy in loads[1] + loads[2]:
        copy.wait()
    gates = jnp.dot(panel[:, 3 * width :], pick_ref[...], preferred_element_type=jnp.float32)
    slots[...] = (gates[:, 1:2] * panel[:, width : 2 * width].astype(jnp.float32)).astype(jnp.bfloat16)
    weights[2].wait()
    for i, repeat in enumerate(repeats):
        store(panel.at[pl.ds(places[i], places[i + 1] - places[i])], repeat)
    keep(panel.at[:, pl.ds(0, width)], rows_out)
    keep(slots, slots_out)
    hidden_grad = contract(slots[...], down_w[...], 1, 1)
    sigma = jax.nn.sigmoid(pre_gate)
    activ = pre_gate * sigma
    hidden[...] = (activ * pre_up).astype(jnp.bfloat16)
    keep(hidden, hidden_out)
    da[...] = (hidden_grad * pre_up * sigma * (1.0 + pre_gate * (1.0 - sigma))).astype(jnp.bfloat16)
    du[...] = (hidden_grad * activ).astype(jnp.bfloat16)
    keep(da, da_out)
    keep(du, du_out)
    back = contract(da[...], gate_w[...], 1, 1) + contract(du[...], up_w[...], 1, 1)
    gain_out[...] = jnp.sum(back * panel[:, :width].astype(jnp.float32), axis=0, keepdims=True)
    back = back.astype(jnp.bfloat16)
    for i in range(count):
        outs[i][:, :width] = back[places[i] : places[i + 1]]
    others = panel[:, 2 * width : 3 * width]
    pre_gate = jnp.dot(others, gate_w[...], preferred_element_type=jnp.float32)
    pre_up = jnp.dot(others, up_w[...], preferred_element_type=jnp.float32)
    ahead = (pre_gate * jax.nn.sigmoid(pre_gate) * pre_up).astype(jnp.bfloat16)
    out = jnp.dot(ahead, down_w[...], preferred_element_type=jnp.float32)
    out = (out * gates[:, 0:1]).astype(jnp.bfloat16)
    for i in range(count):
        outs[i][:, width:] = out[places[i] : places[i + 1]]
    for copy in stores:
        copy.wait()


def run_expert(pieces, gate_w, up_w, down_w, pick, kept, start, total, again=False):
    places = [0]
    for piece in pieces:
        places.append(places[-1] + piece.shape[0])
    rows, (width, hidden) = places[-1], gate_w.shape
    count = len(pieces)
    anywhere = pl.BlockSpec(memory_space=pl.ANY)
    here = pl.BlockSpec(memory_space=pltpu.VMEM)
    bf16 = jnp.bfloat16
    results = pl.pallas_call(
        functools.partial(expert_kernel, tuple(places), start, kept is None, again),
        out_shape=[jax.ShapeDtypeStruct((piece.shape[0], 2 * width), bf16) for piece in pieces]
        + [jax.ShapeDtypeStruct((1, width), jnp.float32)]
        + [jax.ShapeDtypeStruct((total, width), bf16)] * 2
        + [jax.ShapeDtypeStruct((total, hidden), bf16)] * 3
        + [jax.ShapeDtypeStruct(piece.shape, bf16) for piece in pieces if again],
        in_specs=[anywhere] * (count + 3) + [here] + ([] if kept is None else [anywhere] * 5),
        out_specs=[here] * (count + 1) + [anywhere] * (5 + again * count),
        input_output_aliases={} if kept is None else {count + 4 + i: count + 1 + i for i in range(5)},
        scratch_shapes=[
            pltpu.VMEM((rows, pieces[0].shape[1]), bf16),
            pltpu.VMEM((rows, width), bf16),
            pltpu.VMEM((rows, hidden), bf16),
            pltpu.VMEM((rows, hidden), bf16),
            pltpu.VMEM((rows, hidden), bf16),
            pltpu.VMEM(gate_w.shape, bf16),
            pltpu.VMEM(up_w.shape, bf16),
            pltpu.VMEM(down_w.shape, bf16),
            pltpu.SemaphoreType.DMA((3 * count,)),
            pltpu.SemaphoreType.DMA((3,)),
            pltpu.SemaphoreType.DMA((5 + count,)),
        ],
        compiler_params=pltpu.CompilerParams(vmem_limit_bytes=60 * MIB),
        cost_estimate=SMALL,
        name="expert",
    )(*pieces, gate_w, up_w, down_w, pick, *(() if kept is None else kept))
    return results[:count], results[count], results[count + 1 : count + 6], results[count + 6 :]


def nothing(*refs):
    pass


def held_back(arrays, after):
    anywhere = pl.BlockSpec(memory_space=pl.ANY)
    return pl.pallas_call(
        nothing,
        out_shape=[jax.ShapeDtypeStruct(array.shape, array.dtype) for array in arrays],
        in_specs=[anywhere] * (len(arrays) + len(after)),
        out_specs=[anywhere] * len(arrays),
        input_output_aliases={i: i for i in range(len(arrays))},
        cost_estimate=SMALL,
        name="held_back",
    )(*arrays, *after)


def weight_kernel(rows_ref, da_ref, du_ref, hidden_ref, slots_ref, *refs):
    gate_out, up_out, down_out = refs[-3:]
    gate_out[...] = contract(rows_ref[...], da_ref[...], 0, 0).astype(jnp.bfloat16)
    up_out[...] = contract(rows_ref[...], du_ref[...], 0, 0).astype(jnp.bfloat16)
    down_out[...] = contract(hidden_ref[...], slots_ref[...], 0, 0).astype(jnp.bfloat16)


def weight_gradients(kept, after, carried):
    rows, slots, hidden, da, du = kept
    (total, width), inner = rows.shape, da.shape[1]
    block = 2 * LANES
    whole = pl.BlockSpec((total, inner), lambda i: (0, 0))
    part = pl.BlockSpec((total, block), lambda i: (0, i))
    anywhere = pl.BlockSpec(memory_space=pl.ANY)
    waits = len(after)
    results = pl.pallas_call(
        weight_kernel,
        grid=(width // block,),
        out_shape=[jax.ShapeDtypeStruct(piece.shape, piece.dtype) for piece in carried]
        + [jax.ShapeDtypeStruct((width, inner), jnp.bfloat16)] * 2
        + [jax.ShapeDtypeStruct((inner, width), jnp.bfloat16)],
        in_specs=[part, whole, whole, whole, part] + [anywhere] * (waits + len(carried)),
        out_specs=[anywhere] * len(carried)
        + [pl.BlockSpec((block, inner), lambda i: (i, 0))] * 2
        + [pl.BlockSpec((inner, block), lambda i: (0, i))],
        input_output_aliases={5 + waits + i: i for i in range(len(carried))},
        compiler_params=pltpu.CompilerParams(vmem_limit_bytes=56 * MIB),
        cost_estimate=SMALL,
        name="weight_gradients",
    )(rows, da, du, hidden, slots, *after, *carried)
    return results[len(carried) :], results[: len(carried)]


def per_device(
    leaving, returning, saved, gain, w_gate, w_up, w_down, route_a, gates_a, route_b, gates_b
):
    experts = lax.axis_size("expert")
    gain_row = gain[0]
    gate_w = w_gate[0, 0]
    up_w = w_up[0, 0]
    down_w = w_down[0, 0]
    upstream = shifted(returning, "section", -1)[0]
    arrived = shifted(leaving, "section", 1)[0]
    unit, scale, normed_two = normalize(saved[0], gain_row)
    columns = gate_columns(route_a[0], gates_a[0], route_b[0], gates_b[0], experts)
    line = jnp.arange(LANES, dtype=jnp.int32)
    pick = (
        (line[:, None] % experts == lax.axis_index("expert"))
        & (line[:, None] // (3 * experts) == line[None, :])
        & (line[None, :] < 2)
    ).astype(jnp.bfloat16)
    unused_unit, unused_scale, normed_one = normalize(arrived, gain_row)
    near = gather_near(jnp.concatenate([normed_two, upstream, normed_one, columns], axis=1))
    onward = gather_onward(near)
    total = experts * upstream.shape[0]
    expert = functools.partial(
        run_expert, gate_w=gate_w, up_w=up_w, down_w=down_w, pick=pick, total=total
    )
    near_out, gain_near, kept, near = expert(near, kept=None, start=0, again=True)
    staying = gather_staying(near)
    onward_out, gain_onward, kept, onward = expert(onward, kept=kept, start=total // 4, again=True)
    far = gather_far(onward)
    staying_out, gain_staying, kept, unused_pieces = expert(staying, kept=kept, start=total // 2)
    staid = scatter_staying(staying_out)
    far_out, gain_far, kept, unused_pieces = expert(far, kept=kept, start=3 * total // 4)
    far_out = held_back(far_out, staid)
    (grad_gate, grad_up, grad_down), onward_out = weight_gradients(kept, (), onward_out)
    sums = relayed(onward_out, scatter_far(far_out))
    gain_part = (gain_near + gain_onward + gain_staying + gain_far) / gain
    gain_part = ring_sum(
        gain_part, along_x(gain_part, 1), along_x(gain_part, -1), along_x(gain_part, 2)
    )
    returned, gain_total = scatter_sums(near_out, sums, staid, gain_part)
    width = upstream.shape[1]
    normed_grad, gathered = returned[:, :width], returned[:, width:]
    scaled = normed_grad * gain_row
    input_grad = (
        upstream.astype(jnp.float32)
        + scale * (scaled - unit * jnp.mean(scaled * unit, axis=-1, keepdims=True))
    ).astype(jnp.bfloat16)
    mixed = (arrived.astype(jnp.float32) + gathered).astype(jnp.bfloat16)
    return (
        mixed[None],
        input_grad[None],
        grad_gate[None, None],
        grad_up[None, None],
        grad_down[None, None],
        gain_total,
    )


def solution(mesh):
    placed = (
        P("section", "expert", None),
        P("section", "expert", None),
        P("section", "expert", None),
        P("section", None),
        P("section", "expert", None, None),
        P("section", "expert", None, None),
        P("section", "expert", None, None),
        P("section", "expert", None),
        P("section", "expert", None),
        P("section", "expert", None),
        P("section", "expert", None),
    )
    return jax.shard_map(
        per_device,
        mesh=mesh,
        in_specs=placed,
        out_specs=(
            P("section", "expert", None),
            P("section", "expert", None),
            P("section", "expert", None, None),
            P("section", "expert", None, None),
            P("section", "expert", None, None),
            P("section", None),
        ),
        check_vma=False,
    )
```

```python
import functools

import jax
import jax.numpy as jnp
from jax import lax
from jax.experimental import pallas as pl
from jax.experimental.pallas import tpu as pltpu
from jax.sharding import PartitionSpec as P

epsilon = 1e-06
SIDE = 4
LANES = 128
MIB = 1 << 20
SMALL = pl.CostEstimate(flops=1 << 20, bytes_accessed=1 << 16, transcendentals=0)


def shifted(value, axis, steps):
    count = lax.axis_size(axis)
    pairs = [(source, (source + steps) % count) for source in range(count)]
    return lax.ppermute(value, axis, pairs)


def along_x(value, steps):
    pairs = [(z * SIDE + x, z * SIDE + (x + steps) % SIDE) for z in range(SIDE) for x in range(SIDE)]
    return lax.ppermute(value, "expert", pairs)


def along_z(value, steps):
    pairs = [(z * SIDE + x, (z + steps) % SIDE * SIDE + x) for z in range(SIDE) for x in range(SIDE)]
    return lax.ppermute(value, "expert", pairs)


def contract(left, right, left_dim, right_dim):
    return lax.dot_general(
        left, right, (((left_dim,), (right_dim,)), ((), ())), preferred_element_type=jnp.float32
    )


def normalize(panel, gain_row):
    values = panel.astype(jnp.float32)
    scale = lax.rsqrt(jnp.mean(values * values, axis=-1, keepdims=True) + epsilon)
    unit = values * scale
    return (unit, scale, (unit * gain_row).astype(jnp.bfloat16))


def gather_near(block):
    half = block.shape[0] // 2
    part = half // 2
    groups = []
    for own, move in ((block[:half], along_x), (block[half:], along_z)):
        lower, upper = move(own, 1), move(own, -1)
        opposite = (move(lower[:part], 1), move(upper[part:], -1))
        groups += [jnp.concatenate((own, lower), axis=0), jnp.concatenate((upper, *opposite), axis=0)]
    return groups


def gather_onward(near):
    return (along_z(near[0], 1), along_z(near[1], -1), along_x(near[2], 1), along_x(near[3], -1))


def gather_staying(near):
    return (along_z(near[1], 1), along_z(near[0], -1), along_x(near[3], 1), along_x(near[2], -1))


def gather_far(onward):
    return (along_z(onward[0], 1), along_z(onward[1], -1), along_x(onward[2], 1), along_x(onward[3], -1))


def scatter_staying(staying):
    return (along_z(staying[0], -1), along_z(staying[1], 1), along_x(staying[2], -1), along_x(staying[3], 1))


def added(*parts):
    total = parts[0].astype(jnp.float32)
    for part in parts[1:]:
        total = total + part.astype(jnp.float32)
    return total


def ring_sum(own, lower, upper, opposite):
    return (own + opposite) + (lower + upper)


def split(row, count, rows):
    terms = []
    for turn in range(count):
        terms.append(lax.reduce_precision(row, 8, 7))
        row = row - terms[-1]
    return jnp.concatenate(terms).astype(jnp.bfloat16).reshape(rows, -1)


def joined(columns, count):
    terms = columns.astype(jnp.float32).reshape(count, -1)
    total = terms[:1]
    for turn in range(1, count):
        total = total + terms[turn : turn + 1]
    return total


def with_columns(part, columns):
    return jnp.concatenate([part, columns], axis=1)


def scatter_far(far, onward):
    width = onward[0].shape[1]
    got = (
        along_z(far[0], -1), along_z(far[1], 1), along_x(far[2], -1), along_x(far[3], 1)
    )
    brought = got[3][:, width:]
    got = (*got[:3], got[3][:, :width])
    return [added(mine, other).astype(jnp.bfloat16) for mine, other in zip(onward, got)], brought


def scatter_sums(near, sums, staid, extra, brought):
    width = near[0].shape[1]
    back = (
        along_z(sums[0], -1), along_z(sums[1], 1),
        along_x(with_columns(sums[2], extra), -1), along_x(with_columns(sums[3], brought), 1),
    )
    count = extra.size // (width // 2)
    row = ring_sum(*(joined(part, count) for part in (extra, brought, back[2][:, width:], back[3][:, width:])))
    back = (*back[:2], back[2][:, :width], back[3][:, :width])
    totals = (
        added(near[0], back[0], staid[1]),
        added(near[1], back[1], staid[0]),
        added(near[2], back[2], staid[3]),
        added(near[3], back[3], staid[2]),
    )
    rows = totals[0].shape[0] // 2
    terms = split(row, 2, rows)

    def parts(own):
        lower, upper, opposite = own[0][rows:], own[1][:rows], own[1][rows:]
        return own[0][:rows], [part.astype(jnp.bfloat16) for part in (lower, upper, opposite)]

    def ends(sent, move):
        return move(sent[0], -1), move(sent[1], 1), move(sent[2], 2)

    own_first, sent_first = parts(totals[:2])
    own_second, sent_second = parts(totals[2:])
    got_first = ends(sent_first, along_x)
    got_second = ends([with_columns(part, terms) for part in sent_second], along_z)
    result = jnp.concatenate(
        [added(own_first, *got_first), added(own_second, *(part[:, :width] for part in got_second))], axis=0
    )
    upper, lower, opposite = (joined(part[:, width:], 2) for part in got_second)
    return result, ring_sum(joined(terms, 2), lower, upper, opposite)


def gate_columns(route_a, gates_a, route_b, gates_b, experts):
    names = jnp.arange(experts, dtype=jnp.int32)
    columns = []
    for route, gates in ((route_a, gates_a), (route_b, gates_b)):
        dense = jnp.sum(jnp.where(route[:, :, None] == names, gates[:, :, None], 0.0), axis=1)
        for turn in range(3):
            term = lax.reduce_precision(dense, 8, 7)
            columns.append(term.astype(jnp.bfloat16))
            dense = dense - term
    rows = route_a.shape[0]
    columns.append(jnp.zeros((rows, LANES - 6 * experts), jnp.bfloat16))
    return jnp.concatenate(columns, axis=1)


def expert_kernel(places, start, fresh, again, *refs):
    count = len(places) - 1
    pieces = refs[:count]
    gate_hbm, up_hbm, down_hbm, pick_ref = refs[count : count + 4]
    rest = refs[count + 4 + (0 if fresh else 5) :]
    outs = rest[:count]
    gain_out, rows_out, slots_out, hidden_out, da_out, du_out = rest[count : count + 6]
    repeats = rest[count + 6 : 2 * count + 6] if again else ()
    (panel, slots, hidden, da, du, gate_w, up_w, down_w,
     piece_sems, weight_sems, out_sems) = rest[-11:]
    width = gate_w.shape[0]
    def load(part, first, last):
        copies = []
        for i in range(count):
            here, columns = pl.ds(places[i], places[i + 1] - places[i]), pl.ds(first, last - first)
            copies.append(
                pltpu.make_async_copy(
                    pieces[i].at[:, columns], panel.at[here, columns], piece_sems.at[part * count + i]
                )
            )
        return copies

    loads = [load(0, 0, width), load(1, width, 2 * width), load(2, 2 * width, pieces[0].shape[1])]
    weights = [
        pltpu.make_async_copy(source, target, weight_sems.at[i])
        for i, (source, target) in enumerate(((gate_hbm, gate_w), (up_hbm, up_w), (down_hbm, down_w)))
    ]
    stores = []

    def store(source, target):
        copy = pltpu.make_async_copy(source, target, out_sems.at[len(stores)])
        copy.start()
        stores.append(copy)

    def keep(source, target):
        store(source, target.at[pl.ds(start, places[-1])])

    for copy in loads[0] + weights[:1]:
        copy.start()
    for copy in loads[0]:
        copy.wait()
    weights[1].start()
    weights[0].wait()
    for copy in loads[1] + loads[2] + weights[2:]:
        copy.start()
    pre_gate = jnp.dot(panel[:, :width], gate_w[...], preferred_element_type=jnp.float32)
    weights[1].wait()
    pre_up = jnp.dot(panel[:, :width], up_w[...], preferred_element_type=jnp.float32)
    for copy in loads[1] + loads[2]:
        copy.wait()
    gates = jnp.dot(panel[:, 3 * width :], pick_ref[...], preferred_element_type=jnp.float32)
    slots[...] = (gates[:, 1:2] * panel[:, width : 2 * width].astype(jnp.float32)).astype(jnp.bfloat16)
    weights[2].wait()
    for i, repeat in enumerate(repeats):
        store(panel.at[pl.ds(places[i], places[i + 1] - places[i])], repeat)
    keep(panel.at[:, pl.ds(0, width)], rows_out)
    keep(slots, slots_out)
    hidden_grad = contract(slots[...], down_w[...], 1, 1)
    sigma = jax.nn.sigmoid(pre_gate)
    activ = pre_gate * sigma
    hidden[...] = (activ * pre_up).astype(jnp.bfloat16)
    keep(hidden, hidden_out)
    da[...] = (hidden_grad * pre_up * sigma * (1.0 + pre_gate * (1.0 - sigma))).astype(jnp.bfloat16)
    du[...] = (hidden_grad * activ).astype(jnp.bfloat16)
    keep(da, da_out)
    keep(du, du_out)
    back = contract(da[...], gate_w[...], 1, 1) + contract(du[...], up_w[...], 1, 1)
    gain_out[...] = jnp.sum(back * panel[:, :width].astype(jnp.float32), axis=0, keepdims=True)
    back = back.astype(jnp.bfloat16)
    for i in range(count):
        outs[i][:, :width] = back[places[i] : places[i + 1]]
    others = panel[:, 2 * width : 3 * width]
    pre_gate = jnp.dot(others, gate_w[...], preferred_element_type=jnp.float32)
    pre_up = jnp.dot(others, up_w[...], preferred_element_type=jnp.float32)
    ahead = (pre_gate * jax.nn.sigmoid(pre_gate) * pre_up).astype(jnp.bfloat16)
    out = jnp.dot(ahead, down_w[...], preferred_element_type=jnp.float32)
    out = (out * gates[:, 0:1]).astype(jnp.bfloat16)
    for i in range(count):
        outs[i][:, width:] = out[places[i] : places[i + 1]]
    for copy in stores:
        copy.wait()


def run_expert(pieces, gate_w, up_w, down_w, pick, kept, start, total, again=False):
    places = [0]
    for piece in pieces:
        places.append(places[-1] + piece.shape[0])
    rows, (width, hidden) = places[-1], gate_w.shape
    count = len(pieces)
    anywhere = pl.BlockSpec(memory_space=pl.ANY)
    here = pl.BlockSpec(memory_space=pltpu.VMEM)
    bf16 = jnp.bfloat16
    results = pl.pallas_call(
        functools.partial(expert_kernel, tuple(places), start, kept is None, again),
        out_shape=[jax.ShapeDtypeStruct((piece.shape[0], 2 * width), bf16) for piece in pieces]
        + [jax.ShapeDtypeStruct((1, width), jnp.float32)]
        + [jax.ShapeDtypeStruct((total, width), bf16)] * 2
        + [jax.ShapeDtypeStruct((total, hidden), bf16)] * 3
        + [jax.ShapeDtypeStruct(piece.shape, bf16) for piece in pieces if again],
        in_specs=[anywhere] * (count + 3) + [here] + ([] if kept is None else [anywhere] * 5),
        out_specs=[here] * (count + 1) + [anywhere] * (5 + again * count),
        input_output_aliases={} if kept is None else {count + 4 + i: count + 1 + i for i in range(5)},
        scratch_shapes=[
            pltpu.VMEM((rows, pieces[0].shape[1]), bf16),
            pltpu.VMEM((rows, width), bf16),
            pltpu.VMEM((rows, hidden), bf16),
            pltpu.VMEM((rows, hidden), bf16),
            pltpu.VMEM((rows, hidden), bf16),
            pltpu.VMEM(gate_w.shape, bf16),
            pltpu.VMEM(up_w.shape, bf16),
            pltpu.VMEM(down_w.shape, bf16),
            pltpu.SemaphoreType.DMA((3 * count,)),
            pltpu.SemaphoreType.DMA((3,)),
            pltpu.SemaphoreType.DMA((5 + count,)),
        ],
        compiler_params=pltpu.CompilerParams(vmem_limit_bytes=60 * MIB),
        cost_estimate=SMALL,
        name="expert",
    )(*pieces, gate_w, up_w, down_w, pick, *(() if kept is None else kept))
    return results[:count], results[count], results[count + 1 : count + 6], results[count + 6 :]


def nothing(*refs):
    pass


def held_back(arrays, after):
    anywhere = pl.BlockSpec(memory_space=pl.ANY)
    return pl.pallas_call(
        nothing,
        out_shape=[jax.ShapeDtypeStruct(array.shape, array.dtype) for array in arrays],
        in_specs=[anywhere] * (len(arrays) + len(after)),
        out_specs=[anywhere] * len(arrays),
        input_output_aliases={i: i for i in range(len(arrays))},
        cost_estimate=SMALL,
        name="held_back",
    )(*arrays, *after)


def pair_kernel(rows_ref, da_ref, du_ref, *refs):
    gate_out, up_out = refs[-2:]
    gate_out[...] = contract(rows_ref[...], da_ref[...], 0, 0).astype(jnp.bfloat16)
    up_out[...] = contract(rows_ref[...], du_ref[...], 0, 0).astype(jnp.bfloat16)


def single_kernel(slots_ref, hidden_ref, *refs):
    refs[-1][...] = contract(hidden_ref[...], slots_ref[...], 0, 0).astype(jnp.bfloat16)


def products(kernel, parted, whole, out_shape, out_spec, after, carried):
    total, width = parted.shape
    block = 2 * LANES
    anywhere = pl.BlockSpec(memory_space=pl.ANY)
    first = 1 + len(whole) + len(after)
    results = pl.pallas_call(
        kernel,
        grid=(width // block,),
        out_shape=[jax.ShapeDtypeStruct(piece.shape, piece.dtype) for piece in carried]
        + [jax.ShapeDtypeStruct(out_shape, jnp.bfloat16)] * len(whole),
        in_specs=[pl.BlockSpec((total, block), lambda i: (0, i))]
        + [pl.BlockSpec(whole[0].shape, lambda i: (0, 0))] * len(whole)
        + [anywhere] * (len(after) + len(carried)),
        out_specs=[anywhere] * len(carried) + [out_spec(block)] * len(whole),
        input_output_aliases={first + i: i for i in range(len(carried))},
        compiler_params=pltpu.CompilerParams(vmem_limit_bytes=56 * MIB),
        cost_estimate=SMALL,
        name="weight_gradients",
    )(parted, *whole, *after, *carried)
    return results[len(carried) :], results[: len(carried)]


def pair_gradients(rows, da, du, after, carried):
    shape = (rows.shape[1], da.shape[1])
    spec = lambda block: pl.BlockSpec((block, shape[1]), lambda i: (i, 0))
    return products(pair_kernel, rows, (da, du), shape, spec, after, carried)


def single_gradient(slots, hidden, after, carried):
    shape = (hidden.shape[1], slots.shape[1])
    spec = lambda block: pl.BlockSpec((shape[0], block), lambda i: (0, i))
    return products(single_kernel, slots, (hidden,), shape, spec, after, carried)


def per_device(
    leaving, returning, saved, gain, w_gate, w_up, w_down, route_a, gates_a, route_b, gates_b
):
    experts = lax.axis_size("expert")
    gain_row = gain[0]
    gate_w = w_gate[0, 0]
    up_w = w_up[0, 0]
    down_w = w_down[0, 0]
    upstream = shifted(returning, "section", -1)[0]
    arrived = shifted(leaving, "section", 1)[0]
    unit, scale, normed_two = normalize(saved[0], gain_row)
    columns = gate_columns(route_a[0], gates_a[0], route_b[0], gates_b[0], experts)
    line = jnp.arange(LANES, dtype=jnp.int32)
    pick = (
        (line[:, None] % experts == lax.axis_index("expert"))
        & (line[:, None] // (3 * experts) == line[None, :])
        & (line[None, :] < 2)
    ).astype(jnp.bfloat16)
    unused_unit, unused_scale, normed_one = normalize(arrived, gain_row)
    near = gather_near(jnp.concatenate([normed_two, upstream, normed_one, columns], axis=1))
    onward = gather_onward(near)
    rows = upstream.shape[0]
    total = experts * rows
    expert = functools.partial(
        run_expert, gate_w=gate_w, up_w=up_w, down_w=down_w, pick=pick, total=total
    )
    near_out, gain_near, kept, near = expert(near, kept=None, start=0, again=True)
    staying = gather_staying(near)
    onward_out, gain_onward, kept, onward = expert(onward, kept=kept, start=total // 4, again=True)
    far = gather_far(onward)
    staying_out, gain_staying, kept, unused_pieces = expert(staying, kept=kept, start=total // 2)
    staid = scatter_staying(staying_out)
    far_out, gain_far, kept, unused_pieces = expert(far, kept=kept, start=3 * total // 4)
    far_out = held_back(far_out, staid)
    rows_b, slot_grad, hidden, gate_grad, up_grad = kept
    gain_part = (gain_near + gain_onward + gain_staying + gain_far) / gain
    extra = split(gain_part, 4, rows)
    far_out = (*far_out[:3], with_columns(far_out[3], extra))
    (grad_gate, grad_up), onward_out = pair_gradients(rows_b, gate_grad, up_grad, far_out[3:], onward_out)
    sums, brought = scatter_far(far_out, onward_out)
    (grad_down,), near_out = single_gradient(slot_grad, hidden, sums, near_out)
    returned, gain_total = scatter_sums(near_out, sums, staid, extra, brought)
    width = upstream.shape[1]
    normed_grad, gathered = returned[:, :width], returned[:, width:]
    scaled = normed_grad * gain_row
    input_grad = (
        upstream.astype(jnp.float32)
        + scale * (scaled - unit * jnp.mean(scaled * unit, axis=-1, keepdims=True))
    ).astype(jnp.bfloat16)
    mixed = (arrived.astype(jnp.float32) + gathered).astype(jnp.bfloat16)
    return (
        mixed[None],
        input_grad[None],
        grad_gate[None, None],
        grad_up[None, None],
        grad_down[None, None],
        gain_total,
    )


def solution(mesh):
    placed = (
        P("section", "expert", None),
        P("section", "expert", None),
        P("section", "expert", None),
        P("section", None),
        P("section", "expert", None, None),
        P("section", "expert", None, None),
        P("section", "expert", None, None),
        P("section", "expert", None),
        P("section", "expert", None),
        P("section", "expert", None),
        P("section", "expert", None),
    )
    return jax.shard_map(
        per_device,
        mesh=mesh,
        in_specs=placed,
        out_specs=(
            P("section", "expert", None),
            P("section", "expert", None),
            P("section", "expert", None, None),
            P("section", "expert", None, None),
            P("section", "expert", None, None),
            P("section", None),
        ),
        check_vma=False,
    )
```

```python
import functools

import jax
import jax.numpy as jnp
from jax import lax
from jax.experimental import pallas as pl
from jax.experimental.pallas import tpu as pltpu
from jax.sharding import PartitionSpec as P

epsilon = 1e-06
SIDE = 4
LANES = 128
MIB = 1 << 20
SMALL = pl.CostEstimate(flops=1 << 20, bytes_accessed=1 << 16, transcendentals=0)


def shifted(value, axis, steps):
    count = lax.axis_size(axis)
    pairs = [(source, (source + steps) % count) for source in range(count)]
    return lax.ppermute(value, axis, pairs)


def along_x(value, steps):
    pairs = [(z * SIDE + x, z * SIDE + (x + steps) % SIDE) for z in range(SIDE) for x in range(SIDE)]
    return lax.ppermute(value, "expert", pairs)


def along_z(value, steps):
    pairs = [(z * SIDE + x, (z + steps) % SIDE * SIDE + x) for z in range(SIDE) for x in range(SIDE)]
    return lax.ppermute(value, "expert", pairs)


def contract(left, right, left_dim, right_dim):
    return lax.dot_general(
        left, right, (((left_dim,), (right_dim,)), ((), ())), preferred_element_type=jnp.float32
    )


def normalize(panel, gain_row):
    values = panel.astype(jnp.float32)
    scale = lax.rsqrt(jnp.mean(values * values, axis=-1, keepdims=True) + epsilon)
    unit = values * scale
    return (unit, scale, (unit * gain_row).astype(jnp.bfloat16))


def gather_near(block):
    half = block.shape[0] // 2
    part = half // 2
    groups = []
    for own, move in ((block[:half], along_x), (block[half:], along_z)):
        lower, upper = move(own, 1), move(own, -1)
        opposite = (move(lower[:part], 1), move(upper[part:], -1))
        groups += [jnp.concatenate((own, lower), axis=0), jnp.concatenate((upper, *opposite), axis=0)]
    return groups


def gather_onward(near):
    return (along_z(near[0], 1), along_z(near[1], -1), along_x(near[2], 1), along_x(near[3], -1))


def gather_staying(near):
    return (along_z(near[1], 1), along_z(near[0], -1), along_x(near[3], 1), along_x(near[2], -1))


def gather_far(onward):
    return (along_z(onward[0], 1), along_z(onward[1], -1), along_x(onward[2], 1), along_x(onward[3], -1))


def scatter_staying(staying):
    return (along_z(staying[0], -1), along_z(staying[1], 1), along_x(staying[2], -1), along_x(staying[3], 1))


def added(*parts):
    total = parts[0].astype(jnp.float32)
    for part in parts[1:]:
        total = total + part.astype(jnp.float32)
    return total


def ring_sum(own, lower, upper, opposite):
    return (own + opposite) + (lower + upper)


def split(row, count, rows):
    terms = []
    for turn in range(count):
        terms.append(lax.reduce_precision(row, 8, 7))
        row = row - terms[-1]
    return jnp.concatenate(terms).astype(jnp.bfloat16).reshape(rows, -1)


def joined(columns, count):
    terms = columns.astype(jnp.float32).reshape(count, -1)
    total = terms[:1]
    for turn in range(1, count):
        total = total + terms[turn : turn + 1]
    return total


def with_columns(part, columns):
    return jnp.concatenate([part, columns], axis=1)


def scatter_far(far, onward):
    width = onward[0].shape[1]
    got = (
        along_z(far[0], -1), along_z(far[1], 1), along_x(far[2], -1), along_x(far[3], 1)
    )
    brought = got[3][:, width:]
    got = (*got[:3], got[3][:, :width])
    return [added(mine, other).astype(jnp.bfloat16) for mine, other in zip(onward, got)], brought


def scatter_sums(near, sums, staid, extra, brought):
    width = near[0].shape[1]
    back = (along_z(sums[0], -1), along_z(sums[1], 1), along_x(sums[2], -1), along_x(sums[3], 1))
    count = extra.size // (width // 2)
    row = ring_sum(*(joined(part, count) for part in (extra, brought, back[2][:, width:], back[3][:, width:])))
    back = (*back[:2], back[2][:, :width], back[3][:, :width])
    totals = (
        added(near[0], back[0], staid[1]),
        added(near[1], back[1], staid[0]),
        added(near[2], back[2], staid[3]),
        added(near[3], back[3], staid[2]),
    )
    rows = totals[0].shape[0] // 2
    terms = split(row, 2, rows)

    def parts(own):
        lower, upper, opposite = own[0][rows:], own[1][:rows], own[1][rows:]
        return own[0][:rows], [part.astype(jnp.bfloat16) for part in (lower, upper, opposite)]

    def ends(sent, move):
        return move(sent[0], -1), move(sent[1], 1), move(sent[2], 2)

    own_first, sent_first = parts(totals[:2])
    own_second, sent_second = parts(totals[2:])
    got_first = ends(sent_first, along_x)
    got_second = ends([with_columns(part, terms) for part in sent_second], along_z)
    result = jnp.concatenate(
        [added(own_first, *got_first), added(own_second, *(part[:, :width] for part in got_second))], axis=0
    )
    upper, lower, opposite = (joined(part[:, width:], 2) for part in got_second)
    return result, ring_sum(joined(terms, 2), lower, upper, opposite)


def gate_columns(route_a, gates_a, route_b, gates_b, experts):
    names = jnp.arange(experts, dtype=jnp.int32)
    columns = []
    for route, gates in ((route_a, gates_a), (route_b, gates_b)):
        dense = jnp.sum(jnp.where(route[:, :, None] == names, gates[:, :, None], 0.0), axis=1)
        for turn in range(3):
            term = lax.reduce_precision(dense, 8, 7)
            columns.append(term.astype(jnp.bfloat16))
            dense = dense - term
    rows = route_a.shape[0]
    columns.append(jnp.zeros((rows, LANES - 6 * experts), jnp.bfloat16))
    return jnp.concatenate(columns, axis=1)


def expert_kernel(places, start, fresh, again, *refs):
    count = len(places) - 1
    pieces = refs[:count]
    gate_hbm, up_hbm, down_hbm, pick_ref = refs[count : count + 4]
    rest = refs[count + 4 + (0 if fresh else 5) :]
    outs = rest[:count]
    gain_out, rows_out, slots_out, hidden_out, da_out, du_out = rest[count : count + 6]
    repeats = rest[count + 6 : 2 * count + 6] if again else ()
    (panel, slots, hidden, da, du, gate_w, up_w, down_w,
     piece_sems, weight_sems, out_sems) = rest[-11:]
    width = gate_w.shape[0]
    def load(part, first, last):
        copies = []
        for i in range(count):
            here, columns = pl.ds(places[i], places[i + 1] - places[i]), pl.ds(first, last - first)
            copies.append(
                pltpu.make_async_copy(
                    pieces[i].at[:, columns], panel.at[here, columns], piece_sems.at[part * count + i]
                )
            )
        return copies

    loads = [load(0, 0, width), load(1, width, 2 * width), load(2, 2 * width, pieces[0].shape[1])]
    weights = [
        pltpu.make_async_copy(source, target, weight_sems.at[i])
        for i, (source, target) in enumerate(((gate_hbm, gate_w), (up_hbm, up_w), (down_hbm, down_w)))
    ]
    stores = []

    def store(source, target):
        copy = pltpu.make_async_copy(source, target, out_sems.at[len(stores)])
        copy.start()
        stores.append(copy)

    def keep(source, target):
        store(source, target.at[pl.ds(start, places[-1])])

    for copy in loads[0] + weights[:1]:
        copy.start()
    for copy in loads[0]:
        copy.wait()
    weights[1].start()
    weights[0].wait()
    for copy in loads[1] + loads[2] + weights[2:]:
        copy.start()
    pre_gate = jnp.dot(panel[:, :width], gate_w[...], preferred_element_type=jnp.float32)
    weights[1].wait()
    pre_up = jnp.dot(panel[:, :width], up_w[...], preferred_element_type=jnp.float32)
    for copy in loads[1] + loads[2]:
        copy.wait()
    gates = jnp.dot(panel[:, 3 * width :], pick_ref[...], preferred_element_type=jnp.float32)
    slots[...] = (gates[:, 1:2] * panel[:, width : 2 * width].astype(jnp.float32)).astype(jnp.bfloat16)
    weights[2].wait()
    for i, repeat in enumerate(repeats):
        store(panel.at[pl.ds(places[i], places[i + 1] - places[i])], repeat)
    keep(panel.at[:, pl.ds(0, width)], rows_out)
    keep(slots, slots_out)
    hidden_grad = contract(slots[...], down_w[...], 1, 1)
    sigma = jax.nn.sigmoid(pre_gate)
    activ = pre_gate * sigma
    hidden[...] = (activ * pre_up).astype(jnp.bfloat16)
    keep(hidden, hidden_out)
    da[...] = (hidden_grad * pre_up * sigma * (1.0 + pre_gate * (1.0 - sigma))).astype(jnp.bfloat16)
    du[...] = (hidden_grad * activ).astype(jnp.bfloat16)
    keep(da, da_out)
    keep(du, du_out)
    back = contract(da[...], gate_w[...], 1, 1) + contract(du[...], up_w[...], 1, 1)
    gain_out[...] = jnp.sum(back * panel[:, :width].astype(jnp.float32), axis=0, keepdims=True)
    back = back.astype(jnp.bfloat16)
    for i in range(count):
        outs[i][:, :width] = back[places[i] : places[i + 1]]
    others = panel[:, 2 * width : 3 * width]
    pre_gate = jnp.dot(others, gate_w[...], preferred_element_type=jnp.float32)
    pre_up = jnp.dot(others, up_w[...], preferred_element_type=jnp.float32)
    ahead = (pre_gate * jax.nn.sigmoid(pre_gate) * pre_up).astype(jnp.bfloat16)
    out = jnp.dot(ahead, down_w[...], preferred_element_type=jnp.float32)
    out = (out * gates[:, 0:1]).astype(jnp.bfloat16)
    for i in range(count):
        outs[i][:, width:] = out[places[i] : places[i + 1]]
    for copy in stores:
        copy.wait()


def run_expert(pieces, gate_w, up_w, down_w, pick, kept, start, total, again=False):
    places = [0]
    for piece in pieces:
        places.append(places[-1] + piece.shape[0])
    rows, (width, hidden) = places[-1], gate_w.shape
    count = len(pieces)
    anywhere = pl.BlockSpec(memory_space=pl.ANY)
    here = pl.BlockSpec(memory_space=pltpu.VMEM)
    bf16 = jnp.bfloat16
    results = pl.pallas_call(
        functools.partial(expert_kernel, tuple(places), start, kept is None, again),
        out_shape=[jax.ShapeDtypeStruct((piece.shape[0], 2 * width), bf16) for piece in pieces]
        + [jax.ShapeDtypeStruct((1, width), jnp.float32)]
        + [jax.ShapeDtypeStruct((total, width), bf16)] * 2
        + [jax.ShapeDtypeStruct((total, hidden), bf16)] * 3
        + [jax.ShapeDtypeStruct(piece.shape, bf16) for piece in pieces if again],
        in_specs=[anywhere] * (count + 3) + [here] + ([] if kept is None else [anywhere] * 5),
        out_specs=[here] * (count + 1) + [anywhere] * (5 + again * count),
        input_output_aliases={} if kept is None else {count + 4 + i: count + 1 + i for i in range(5)},
        scratch_shapes=[
            pltpu.VMEM((rows, pieces[0].shape[1]), bf16),
            pltpu.VMEM((rows, width), bf16),
            pltpu.VMEM((rows, hidden), bf16),
            pltpu.VMEM((rows, hidden), bf16),
            pltpu.VMEM((rows, hidden), bf16),
            pltpu.VMEM(gate_w.shape, bf16),
            pltpu.VMEM(up_w.shape, bf16),
            pltpu.VMEM(down_w.shape, bf16),
            pltpu.SemaphoreType.DMA((3 * count,)),
            pltpu.SemaphoreType.DMA((3,)),
            pltpu.SemaphoreType.DMA((5 + count,)),
        ],
        compiler_params=pltpu.CompilerParams(vmem_limit_bytes=60 * MIB),
        cost_estimate=SMALL,
        name="expert",
    )(*pieces, gate_w, up_w, down_w, pick, *(() if kept is None else kept))
    return results[:count], results[count], results[count + 1 : count + 6], results[count + 6 :]


def nothing(*refs):
    pass


def held_back(arrays, after):
    anywhere = pl.BlockSpec(memory_space=pl.ANY)
    return pl.pallas_call(
        nothing,
        out_shape=[jax.ShapeDtypeStruct(array.shape, array.dtype) for array in arrays],
        in_specs=[anywhere] * (len(arrays) + len(after)),
        out_specs=[anywhere] * len(arrays),
        input_output_aliases={i: i for i in range(len(arrays))},
        cost_estimate=SMALL,
        name="held_back",
    )(*arrays, *after)


def pair_kernel(rows_ref, da_ref, du_ref, *refs):
    gate_out, up_out = refs[-2:]
    gate_out[...] = contract(rows_ref[...], da_ref[...], 0, 0).astype(jnp.bfloat16)
    up_out[...] = contract(rows_ref[...], du_ref[...], 0, 0).astype(jnp.bfloat16)


def single_kernel(slots_ref, hidden_ref, *refs):
    refs[-1][...] = contract(hidden_ref[...], slots_ref[...], 0, 0).astype(jnp.bfloat16)


def products(kernel, parted, whole, out_shape, out_spec, after, carried):
    total, width = parted.shape
    block = 2 * LANES
    anywhere = pl.BlockSpec(memory_space=pl.ANY)
    first = 1 + len(whole) + len(after)
    results = pl.pallas_call(
        kernel,
        grid=(width // block,),
        out_shape=[jax.ShapeDtypeStruct(piece.shape, piece.dtype) for piece in carried]
        + [jax.ShapeDtypeStruct(out_shape, jnp.bfloat16)] * len(whole),
        in_specs=[pl.BlockSpec((total, block), lambda i: (0, i))]
        + [pl.BlockSpec(whole[0].shape, lambda i: (0, 0))] * len(whole)
        + [anywhere] * (len(after) + len(carried)),
        out_specs=[anywhere] * len(carried) + [out_spec(block)] * len(whole),
        input_output_aliases={first + i: i for i in range(len(carried))},
        compiler_params=pltpu.CompilerParams(vmem_limit_bytes=56 * MIB),
        cost_estimate=SMALL,
        name="weight_gradients",
    )(parted, *whole, *after, *carried)
    return results[len(carried) :], results[: len(carried)]


def pair_gradients(rows, da, du, after, carried):
    shape = (rows.shape[1], da.shape[1])
    spec = lambda block: pl.BlockSpec((block, shape[1]), lambda i: (i, 0))
    return products(pair_kernel, rows, (da, du), shape, spec, after, carried)


def single_gradient(slots, hidden, after, carried):
    shape = (hidden.shape[1], slots.shape[1])
    spec = lambda block: pl.BlockSpec((shape[0], block), lambda i: (0, i))
    return products(single_kernel, slots, (hidden,), shape, spec, after, carried)


def per_device(
    leaving, returning, saved, gain, w_gate, w_up, w_down, route_a, gates_a, route_b, gates_b
):
    experts = lax.axis_size("expert")
    gain_row = gain[0]
    gate_w = w_gate[0, 0]
    up_w = w_up[0, 0]
    down_w = w_down[0, 0]
    upstream = shifted(returning, "section", -1)[0]
    arrived = shifted(leaving, "section", 1)[0]
    unit, scale, normed_two = normalize(saved[0], gain_row)
    columns = gate_columns(route_a[0], gates_a[0], route_b[0], gates_b[0], experts)
    line = jnp.arange(LANES, dtype=jnp.int32)
    pick = (
        (line[:, None] % experts == lax.axis_index("expert"))
        & (line[:, None] // (3 * experts) == line[None, :])
        & (line[None, :] < 2)
    ).astype(jnp.bfloat16)
    unused_unit, unused_scale, normed_one = normalize(arrived, gain_row)
    near = gather_near(jnp.concatenate([normed_two, upstream, normed_one, columns], axis=1))
    onward = gather_onward(near)
    rows = upstream.shape[0]
    total = experts * rows
    expert = functools.partial(
        run_expert, gate_w=gate_w, up_w=up_w, down_w=down_w, pick=pick, total=total
    )
    near_out, gain_near, kept, near = expert(near, kept=None, start=0, again=True)
    staying = gather_staying(near)
    onward_out, gain_onward, kept, onward = expert(onward, kept=kept, start=total // 4, again=True)
    far = gather_far(onward)
    staying_out, gain_staying, kept, unused_pieces = expert(staying, kept=kept, start=total // 2)
    staid = scatter_staying(staying_out)
    far_out, gain_far, kept, unused_pieces = expert(far, kept=kept, start=3 * total // 4)
    far_out = held_back(far_out, staid)
    rows_b, slot_grad, hidden, gate_grad, up_grad = kept
    gain_part = (gain_near + gain_onward + gain_staying + gain_far) / gain
    extra = split(gain_part, 4, rows)
    far_out = (*far_out[:3], with_columns(far_out[3], extra))
    (grad_gate, grad_up), onward_out = pair_gradients(rows_b, gate_grad, up_grad, far_out[3:], onward_out)
    sums, brought = scatter_far(far_out, onward_out)
    wide = (with_columns(sums[2], extra), with_columns(sums[3], brought))
    sums = (*held_back(sums[:2], wide), *wide)
    (grad_down,), near_out = single_gradient(slot_grad, hidden, sums, near_out)
    returned, gain_total = scatter_sums(near_out, sums, staid, extra, brought)
    width = upstream.shape[1]
    normed_grad, gathered = returned[:, :width], returned[:, width:]
    scaled = normed_grad * gain_row
    input_grad = (
        upstream.astype(jnp.float32)
        + scale * (scaled - unit * jnp.mean(scaled * unit, axis=-1, keepdims=True))
    ).astype(jnp.bfloat16)
    mixed = (arrived.astype(jnp.float32) + gathered).astype(jnp.bfloat16)
    return (
        mixed[None],
        input_grad[None],
        grad_gate[None, None],
        grad_up[None, None],
        grad_down[None, None],
        gain_total,
    )


def solution(mesh):
    placed = (
        P("section", "expert", None),
        P("section", "expert", None),
        P("section", "expert", None),
        P("section", None),
        P("section", "expert", None, None),
        P("section", "expert", None, None),
        P("section", "expert", None, None),
        P("section", "expert", None),
        P("section", "expert", None),
        P("section", "expert", None),
        P("section", "expert", None),
    )
    return jax.shard_map(
        per_device,
        mesh=mesh,
        in_specs=placed,
        out_specs=(
            P("section", "expert", None),
            P("section", "expert", None),
            P("section", "expert", None, None),
            P("section", "expert", None, None),
            P("section", "expert", None, None),
            P("section", None),
        ),
        check_vma=False,
    )
```
